512 devices in a mesh: client: 32 (over z_hi, x, core), tensor: 16 (over z_lo, y).
Axes of the slice: x: 4, y: 4, z: 16 (z_hi: 4, z_lo: 4; z = z_hi * 4 + z_lo), core: 2. Of those that a mesh axis runs over, the one named last changes fastest.
Arguments:
- tokens: bfloat16 [8192, 8192], P('client', 'tensor'), may hold values from -40 to 40, as said below
- norm_gain: float32 [8192], replicated, may hold values from 0.25 to 1.75
- base_weight: bfloat16 [8192, 8192], P('client', 'tensor'), may hold values from -0.0625 to 0.0625
- factor_a: bfloat16 [2048, 8192], P(('client', 'tensor')), may hold values from -0.0625 to 0.0625
- factor_b: bfloat16 [8192, 2048], P('tensor', 'client'), may hold values from -0.0625 to 0.0625
Outputs:
- query: bfloat16 [8192, 8192], P('client', 'tensor')
The draws below stay inside these ranges and needn't reach their ends.
Inputs may be any that keep to these rules, and one draw needn't show every extreme that they name: tokens: real-valued hidden states.
All inputs are finite; a program needn't handle non-finite values.
Results may differ from the reference program's by a relative error of at most 0.014.
Values may be sent and summed in bfloat16 or wider, within the bound.
No kernel may reach another device: no remote copies, remote signals or barrier semaphores. Data moves between devices by JAX's collectives and lax.ppermute only.
A program may use at most 64 MiB of HBM per device.

```python
import jax
import jax.numpy as jnp
from jax import lax

D = 8192
Q = 8192
TOKENS = 8192
STACK = 2048


def draw_tokens(key, part):
    key = jax.random.fold_in(key, 11)
    key_col, key_row, key_base = jax.random.split(key, 3)
    col_scale = jnp.exp(jax.random.uniform(key_col, (D,), jnp.float32, -1.15, 1.15))
    row_scale = jnp.exp(jax.random.uniform(key_row, (TOKENS, 1), jnp.float32, -1.15, 1.15))
    base = jnp.clip(jax.random.normal(key_base, (TOKENS, D), jnp.float32), -3.9, 3.9)
    return (base * col_scale * row_scale).astype(jnp.bfloat16)


def shard_levels(own_key, dims, cuts, smallest, top_value):
    def one(dim, parts):
        steps = jax.random.uniform(jax.random.fold_in(jax.random.fold_in(own_key, 6), dim), (parts,), jnp.float32, smallest / len(cuts), top_value / len(cuts))
        return jnp.repeat(jnp.exp(steps), dims[dim] // parts).reshape((-1,) + (1,) * (len(dims) - dim - 1))

    factor_of = one(*cuts[0])
    for cut in cuts[1:]:
        factor_of = factor_of * one(*cut)
    return factor_of


def noise(stream_key, dims, scale, reach, cuts=(), kind=jnp.bfloat16):
    array = scale * jax.random.normal(stream_key, dims, jnp.float32)
    if cuts:
        array = array * shard_levels(stream_key, dims, cuts, -0.22, 0.18)
    return jnp.clip(array, -reach, reach).astype(kind)


def setup_inputs(seed: int = 0) -> dict:
    streams_of = jax.random.split(jax.random.key(seed), 6)
    return {
        "tokens": draw_tokens(jax.random.fold_in(streams_of[5], 71), 0),
        "norm_gain": jnp.clip(1.0 + 0.15 * jax.random.normal(streams_of[1], (D,), jnp.float32), 0.25, 1.75),
        "base_weight": noise(streams_of[2], (D, Q), D ** -0.5, 0.0625, ((0, 32), (1, 16))),
        "factor_a": noise(streams_of[3], (STACK, D), D ** -0.5, 0.0625, ((0, 512),)),
        "factor_b": noise(streams_of[4], (Q, STACK), (4 * STACK) ** -0.5, 0.0625, ((0, 16), (1, 32))),
    }


adapter_scale = 2.0
norm_epsilon = 1e-05

def reference(tokens, norm_gain, base_weight, factor_a, factor_b):
    values = tokens.astype(jnp.float32)
    mean_square = lax.optimization_barrier(jnp.mean(values * values, axis=-1, keepdims=True))
    normed = (values * lax.rsqrt(mean_square + norm_epsilon) * norm_gain.astype(jnp.float32)).astype(jnp.bfloat16)
    factor_product = lax.dot_general(factor_a, factor_b, (((0,), (1,)), ((), ())), preferred_element_type=jnp.float32)
    weight_update = lax.optimization_barrier((adapter_scale * factor_product).astype(jnp.bfloat16))
    merged = (base_weight.astype(jnp.float32) + weight_update.astype(jnp.float32)).astype(jnp.bfloat16)
    return jnp.dot(normed, merged, preferred_element_type=jnp.float32).astype(jnp.bfloat16)
```

```python
import jax
import jax.numpy as jnp
from jax import lax
from jax.sharding import Mesh, PartitionSpec as P

adapter_scale = 2.0
norm_epsilon = 1e-05
width = 8192

f32 = jnp.float32
bf16 = jnp.bfloat16


def spread(block, axes, count):
    copies = jnp.broadcast_to(block[None], (count,) + block.shape)
    return lax.all_to_all(copies, axes, split_axis=0, concat_axis=0)


def swap(block):
    return lax.ppermute(block, "core", [(0, 1), (1, 0)])


def turn(block, axis, step):
    return lax.ppermute(block, axis, [(i, (i + step) % 4) for i in range(4)])


def local(tokens, norm_gain, base_weight, factor_a, factor_b):
    core = lax.axis_index("core")
    z_hi = lax.axis_index("z_hi")
    client = (z_hi * 4 + lax.axis_index("x")) * 2 + core

    keep = lax.dynamic_slice_in_dim(tokens, core * 256, 256, axis=1)
    give = lax.dynamic_slice_in_dim(tokens, (1 - core) * 256, 256, axis=1)
    pair = jnp.concatenate([keep, swap(give)], axis=0)
    rows = lax.all_gather(pair, ("z_lo", "y"), axis=1, tiled=True)

    up = factor_b.T
    up = spread(up, "z_hi", 4)
    up = spread(up, "x", 4)
    down = factor_a.reshape(4, 16, 512).transpose(1, 0, 2)
    down = lax.all_to_all(down, ("z_hi", "x"), split_axis=0, concat_axis=0)
    down = spread(down, "z_lo", 4)
    down = spread(down, "y", 4)
    up = up.reshape(4, 4, 4, 4, 4, 512).transpose(3, 2, 1, 0, 4, 5).reshape(1024, 512)
    down = down.reshape(1024, 512)
    part = lax.dot_general(down, up, (((0,), (0,)), ((), ())), preferred_element_type=f32)
    mine = lax.dynamic_slice_in_dim(part, core * 256, 256, axis=0)
    other = lax.dynamic_slice_in_dim(part, (1 - core) * 256, 256, axis=0).astype(bf16)
    update = mine + swap(other).astype(f32)
    gain = lax.dynamic_slice_in_dim(norm_gain, client * 256, 256)[:, None]
    weight = (gain * (base_weight.astype(f32) + adapter_scale * update)).astype(bf16)

    blocks = [weight] + [turn(weight, "z_hi", step) for step in (1, 3, 2)]
    wide = [spread(block, "x", 4) for block in blocks]

    squares = rows.astype(f32)
    squares = jnp.sum(squares * squares, axis=1)
    total = squares[:256] + swap(squares[256:])
    scale = lax.rsqrt(total / width + norm_epsilon)

    acc = None
    for step, block in zip((0, 1, 3, 2), wide):
        source = lax.rem(z_hi + 4 - step, 4)
        left = lax.dynamic_slice_in_dim(rows, source * 1024, 1024, axis=1)
        term = jnp.dot(left, block.reshape(1024, 512), preferred_element_type=f32)
        acc = term if acc is None else acc + term
    query = acc[:256] + swap(acc[256:].astype(bf16)).astype(f32)
    return (query * scale[:, None]).astype(bf16)


def solution(mesh):
    fine = Mesh(mesh.devices.reshape(4, 4, 2, 4, 4), ("z_hi", "x", "core", "z_lo", "y"))
    client, tensor = ("z_hi", "x", "core"), ("z_lo", "y")
    return jax.shard_map(
        local,
        mesh=fine,
        in_specs=(
            P(client, tensor),
            P(),
            P(client, tensor),
            P(client + tensor, None),
            P(tensor, client),
        ),
        out_specs=P(client, tensor),
        check_vma=False,
    )
```

```python
import jax
import jax.numpy as jnp
from jax import lax
from jax.experimental import pallas as pl
from jax.experimental.pallas import tpu as pltpu
from jax.sharding import Mesh, PartitionSpec as P

adapter_scale = 2.0
norm_epsilon = 1e-05
width = 8192

f32 = jnp.float32
bf16 = jnp.bfloat16


def exchange(blocks, axis):
    return lax.all_to_all(blocks, axis, split_axis=0, concat_axis=0)


def copies(block):
    return jnp.broadcast_to(block[None], (4,) + block.shape)


def ahead(block, axis, step):
    return lax.ppermute(block, axis, [(i, (i - step) % 4) for i in range(4)])


def ring(block, axis):
    blocks = [block] + [ahead(block, axis, r) for r in (1, 2, 3)]
    return lax.dynamic_slice_in_dim(
        jnp.stack(blocks + blocks), lax.rem(4 - lax.axis_index(axis), 4), 4, axis=0
    )


def swap(block):
    return lax.ppermute(block, "core", [(0, 1), (1, 0)])


def mirror(block, flip):
    pairs = [
        ((i * 2 + c) * 4 + j, (j * 2 + (c ^ flip)) * 4 + i)
        for i in range(4)
        for c in range(2)
        for j in range(4)
    ]
    return lax.ppermute(block, ("x", "core", "y"), pairs)


def thirds(value):
    parts = []
    for _ in range(3):
        part = lax.reduce_precision(value, 8, 7)
        parts.append(part.astype(bf16))
        value = value - part
    return jnp.stack(parts)


def product_kernel(place, rows, own, after, before, far_a, far_b, keep, give):
    far = jnp.concatenate([far_a[...], far_b[...]], axis=0)
    weights = [own[...], after[...], far, before[...]]

    def block(r, carry):
        y = lax.rem(place[1] + r, 4)
        for core, out in ((0, keep), (1, give)):
            total = None
            for step in range(4):
                z = lax.rem(place[0] + step, 4)
                left = rows[y, z, :256, core * 256 : core * 256 + 256]
                term = jnp.dot(left, weights[step], preferred_element_type=f32)
                total = term if total is None else total + term
            out[r] = total.astype(out.dtype)
        return carry

    lax.fori_loop(0, 4, block, 0)


def product(place, rows, own, after, before, far_a, far_b):
    vmem = pl.BlockSpec(memory_space=pltpu.VMEM)
    return pl.pallas_call(
        product_kernel,
        out_shape=(
            jax.ShapeDtypeStruct((4, 256, 512), f32),
            jax.ShapeDtypeStruct((4, 256, 512), bf16),
        ),
        in_specs=[pl.BlockSpec(memory_space=pltpu.SMEM)] + [vmem] * 6,
        out_specs=(vmem, vmem),
        compiler_params=pltpu.CompilerParams(vmem_limit_bytes=40 * 2**20),
        cost_estimate=pl.CostEstimate(
            flops=2 * 2048 * 1024 * 512, bytes_accessed=9 * 2**20, transcendentals=0
        ),
    )(place, rows, own, after, before, far_a, far_b)


def local(tokens, norm_gain, base_weight, factor_a, factor_b):
    core = lax.axis_index("core")
    z_hi, x = lax.axis_index("z_hi"), lax.axis_index("x")
    client = (z_hi * 4 + x) * 2 + core

    keep = lax.dynamic_slice_in_dim(tokens, core * 256, 256, axis=1)
    give = lax.dynamic_slice_in_dim(tokens, (1 - core) * 256, 256, axis=1)
    values = tokens.astype(f32)
    squares = thirds(jnp.sum(values * values, axis=1))
    squares = jnp.pad(squares, ((0, 13), (0, 256)))
    pair = jnp.concatenate([mirror(keep, 0), mirror(give, 1)], axis=1)

    down = factor_a.reshape(4, 4, 4, 512).transpose(1, 2, 0, 3).reshape(4, 16, 512)
    both = exchange(jnp.concatenate([copies(factor_b.T), down], axis=1), "z_hi")
    up = both[:, :64]
    down = both[:, 64:].reshape(4, 4, 4, 512).transpose(1, 0, 2, 3).reshape(64, 512)
    line = copies(jnp.concatenate([pair, squares, down], axis=0))
    line, up = lax.optimization_barrier((line, up))

    line = exchange(line, "z_lo")
    up = ring(up, "x")
    down = line[:, 272:].reshape(4, 4, 16, 512).transpose(1, 0, 2, 3)
    down = jnp.broadcast_to(down[:, None], (4, 4, 4, 16, 512)).reshape(16, 64, 512)
    line, up, down = lax.optimization_barrier((line, up, down))

    down = exchange(down, ("x", "y"))
    up = up.reshape(4, 4, 4, 4, 4, 512).transpose(0, 3, 2, 1, 4, 5).reshape(1024, 512)
    rows = copies(line[:, :272])
    rows, up, down = lax.optimization_barrier((rows, up, down))

    rows = exchange(rows, "y")
    part = lax.dot_general(
        down.reshape(1024, 512), up, (((0,), (0,)), ((), ())), preferred_element_type=f32
    )
    mine = lax.dynamic_slice_in_dim(part, core * 256, 256, axis=0)
    other = lax.dynamic_slice_in_dim(part, (1 - core) * 256, 256, axis=0).astype(bf16)
    update = mine + swap(other).astype(f32)
    gain = lax.dynamic_slice_in_dim(norm_gain, client * 256, 256)[:, None]
    weight = (gain * (base_weight.astype(f32) + adapter_scale * update)).astype(bf16)

    after, before = ahead(weight, "z_hi", 1), ahead(weight, "z_hi", 3)
    far_a, far_b = ahead(after[:128], "z_hi", 1), ahead(before[128:], "z_hi", 3)
    keep, give = product(jnp.stack([z_hi, x]), rows, weight, after, before, far_a, far_b)

    sums = keep + swap(give).astype(f32)
    query = sums[0]
    for r in (1, 2, 3):
        query = query + ahead(sums[r].astype(bf16), "x", 4 - r).astype(f32)
    squares = jnp.sum(rows[:, :, 256:259, :256].astype(f32), axis=(0, 1, 2))
    scale = lax.rsqrt(squares / width + norm_epsilon)
    return (query * scale[:, None]).astype(bf16)


def solution(mesh):
    fine = Mesh(mesh.devices.reshape(4, 4, 2, 4, 4), ("z_hi", "x", "core", "z_lo", "y"))
    client, tensor = ("z_hi", "x", "core"), ("z_lo", "y")
    return jax.shard_map(
        local,
        mesh=fine,
        in_specs=(
            P(client, tensor),
            P(),
            P(client, tensor),
            P(client + tensor, None),
            P(tensor, client),
        ),
        out_specs=P(client, tensor),
        check_vma=False,
    )
```

```python
import jax
import jax.numpy as jnp
from jax import lax
from jax.experimental import pallas as pl
from jax.experimental.pallas import tpu as pltpu
from jax.sharding import Mesh, PartitionSpec as P

adapter_scale = 2.0
norm_epsilon = 1e-05
width = 8192

f32 = jnp.float32
bf16 = jnp.bfloat16


def exchange(blocks, axis):
    return lax.all_to_all(blocks, axis, split_axis=0, concat_axis=0)


def copies(block):
    return jnp.broadcast_to(block[None], (4,) + block.shape)


def ahead(block, axis, step):
    return lax.ppermute(block, axis, [(i, (i - step) % 4) for i in range(4)])


def turned(blocks, axis):
    return lax.dynamic_slice_in_dim(
        jnp.stack(blocks + blocks), lax.rem(4 - lax.axis_index(axis), 4), 4, axis=0
    )


def swap(block):
    return lax.ppermute(block, "core", [(0, 1), (1, 0)])


def mirror(block, flip):
    pairs = [
        ((i * 2 + c) * 4 + j, (j * 2 + (c ^ flip)) * 4 + i)
        for i in range(4)
        for c in range(2)
        for j in range(4)
    ]
    return lax.ppermute(block, ("x", "core", "y"), pairs)


def thirds(value):
    parts = []
    for _ in range(3):
        part = lax.reduce_precision(value, 8, 7)
        parts.append(part.astype(bf16))
        value = value - part
    return jnp.stack(parts)


def line_kernel(own, first, second, third, out):
    for z, block in enumerate((own, first, second, third)):
        value = block[...]
        for y in range(4):
            out[y, z] = value


def line_copies(*blocks):
    vmem = pl.BlockSpec(memory_space=pltpu.VMEM)
    return pl.pallas_call(
        line_kernel,
        out_shape=jax.ShapeDtypeStruct((4, 4) + blocks[0].shape, bf16),
        in_specs=[vmem] * 4,
        out_specs=vmem,
        compiler_params=pltpu.CompilerParams(vmem_limit_bytes=40 * 2**20),
        cost_estimate=pl.CostEstimate(flops=0, bytes_accessed=6 * 2**20, transcendentals=0),
    )(*blocks)


def product_kernel(place, rows, own, after_a, after_b, before_a, before_b, far_a, far_b, out, weights):
    weights[0] = own[...]
    for step, (upper, lower) in enumerate(
        ((after_a, after_b), (far_a, far_b), (before_a, before_b)), start=1
    ):
        weights[step, :128] = upper[...]
        weights[step, 128:] = lower[...]
    columns = 256 if out.dtype == bf16 else 0
    for y in range(4):
        total = None
        for z in range(4):
            left = rows[y, z, :256, columns : columns + 256]
            right = weights[lax.rem(place[0] + z, 4)]
            term = jnp.dot(left, right, preferred_element_type=f32)
            total = term if total is None else total + term
        out[lax.rem(place[1] + y, 4)] = total.astype(out.dtype)


def product(kind, place, rows, *weights):
    vmem = pl.BlockSpec(memory_space=pltpu.VMEM)
    return pl.pallas_call(
        product_kernel,
        out_shape=jax.ShapeDtypeStruct((4, 256, 512), kind),
        in_specs=[pl.BlockSpec(memory_space=pltpu.SMEM)] + [vmem] * 8,
        out_specs=vmem,
        scratch_shapes=[pltpu.VMEM((4, 256, 512), bf16)],
        compiler_params=pltpu.CompilerParams(vmem_limit_bytes=40 * 2**20),
        cost_estimate=pl.CostEstimate(
            flops=2048 * 1024 * 512, bytes_accessed=7 * 2**20, transcendentals=0
        ),
    )(place, rows, *weights)


def message_kernel(up, down, out):
    for z in range(4):
        out[z, :64] = up[...]
        out[z, 64:] = jnp.concatenate(
            [down[:, z * 2048 + x * 512 : z * 2048 + x * 512 + 512] for x in range(4)], axis=0
        )


def message(up, down):
    vmem = pl.BlockSpec(memory_space=pltpu.VMEM)
    return pl.pallas_call(
        message_kernel,
        out_shape=jax.ShapeDtypeStruct((4, 80, 512), bf16),
        in_specs=[vmem] * 2,
        out_specs=vmem,
        cost_estimate=pl.CostEstimate(flops=0, bytes_accessed=2**19, transcendentals=0),
    )(up, down)


def local(tokens, norm_gain, base_weight, factor_a, factor_b):
    core = lax.axis_index("core")
    z_hi, x = lax.axis_index("z_hi"), lax.axis_index("x")
    z_lo = lax.axis_index("z_lo")
    client = (z_hi * 4 + x) * 2 + core

    keep = lax.dynamic_slice_in_dim(tokens, core * 256, 256, axis=1)
    give = lax.dynamic_slice_in_dim(tokens, (1 - core) * 256, 256, axis=1)
    values = tokens.astype(f32)
    squares = thirds(jnp.sum(values * values, axis=1))
    squares = jnp.pad(squares, ((0, 13), (0, 256)))
    pair = jnp.concatenate([mirror(keep, 0), mirror(give, 1)], axis=1)

    both = exchange(message(factor_b.T, factor_a), "z_hi")
    up = both[:, :64]
    down = both[:, 64:].reshape(4, 4, 4, 512).transpose(1, 0, 2, 3).reshape(64, 512)
    pair = jnp.concatenate([pair, squares], axis=0)
    pair, up, down = lax.optimization_barrier((pair, up, copies(down)))

    rows = [ahead(pair, "z_lo", r) for r in (1, 3)]
    ups = [ahead(up, "x", r) for r in (1, 3)]
    down = exchange(down, "z_lo").reshape(4, 4, 16, 512).transpose(1, 0, 2, 3)
    down = jnp.broadcast_to(down[:, None], (4, 4, 4, 16, 512)).reshape(16, 64, 512)
    rows, ups, down = lax.optimization_barrier((rows, ups, down))

    rows = line_copies(pair, rows[0], ahead(pair, "z_lo", 2), rows[1])
    down = exchange(down, ("x", "y"))
    up = turned([up, ups[0], ahead(up, "x", 2), ups[1]], "x").reshape(4, 4, 4, 4, 4, 512).transpose(0, 3, 2, 1, 4, 5).reshape(1024, 512)
    rows, up, down = lax.optimization_barrier((rows, up, down))

    rows = exchange(rows, "y")
    part = lax.dot_general(
        down.reshape(1024, 512), up, (((0,), (0,)), ((), ())), preferred_element_type=f32
    )
    mine = lax.dynamic_slice_in_dim(part, core * 256, 256, axis=0)
    other = lax.dynamic_slice_in_dim(part, (1 - core) * 256, 256, axis=0).astype(bf16)
    update = mine + swap(other).astype(f32)
    gain = lax.dynamic_slice_in_dim(norm_gain, client * 256, 256)[:, None]
    weight = (gain * (base_weight.astype(f32) + adapter_scale * update)).astype(bf16)

    upper, lower = weight[:128], weight[128:]
    after_a, before_b = ahead(upper, "z_hi", 1), ahead(lower, "z_hi", 3)
    after_b, before_a = ahead(lower, "z_hi", 1), ahead(upper, "z_hi", 3)
    far_a, far_b = ahead(after_a, "z_hi", 1), ahead(before_b, "z_hi", 3)
    place = jnp.stack([lax.rem(z_lo + 4 - z_hi, 4), 4 - x])
    weights = (weight, after_a, after_b, before_a, before_b, far_a, far_b)
    give = product(bf16, place, rows, *weights)
    keep = product(f32, place, rows, *weights)

    sums = keep + swap(give).astype(f32)
    query = sums[0]
    for r in (1, 2, 3):
        query = query + ahead(sums[r].astype(bf16), "x", 4 - r).astype(f32)
    squares = jnp.sum(rows[:, :, 256:259, :256].astype(f32), axis=(0, 1, 2))
    scale = lax.rsqrt(squares / width + norm_epsilon)
    return (query * scale[:, None]).astype(bf16)


def solution(mesh):
    fine = Mesh(mesh.devices.reshape(4, 4, 2, 4, 4), ("z_hi", "x", "core", "z_lo", "y"))
    client, tensor = ("z_hi", "x", "core"), ("z_lo", "y")
    return jax.shard_map(
        local,
        mesh=fine,
        in_specs=(
            P(client, tensor),
            P(),
            P(client, tensor),
            P(client + tensor, None),
            P(tensor, client),
        ),
        out_specs=P(client, tensor),
        check_vma=False,
    )
```

```python
import jax
import jax.numpy as jnp
from jax import lax
from jax.experimental import pallas as pl
from jax.experimental.pallas import tpu as pltpu
from jax.sharding import Mesh, PartitionSpec as P

adapter_scale = 2.0
norm_epsilon = 1e-05
width = 8192

f32 = jnp.float32
bf16 = jnp.bfloat16


def exchange(blocks, axis):
    return lax.all_to_all(blocks, axis, split_axis=0, concat_axis=0)


def copies(block):
    return jnp.broadcast_to(block[None], (4,) + block.shape)


def ahead(block, axis, step):
    return lax.ppermute(block, axis, [(i, (i - step) % 4) for i in range(4)])


def turned(blocks, axis):
    return lax.dynamic_slice_in_dim(
        jnp.stack(blocks + blocks), lax.rem(4 - lax.axis_index(axis), 4), 4, axis=0
    )


def swap(block):
    return lax.ppermute(block, "core", [(0, 1), (1, 0)])


def mirror(block, flip):
    pairs = [
        ((i * 2 + c) * 4 + j, (j * 2 + (c ^ flip)) * 4 + i)
        for i in range(4)
        for c in range(2)
        for j in range(4)
    ]
    return lax.ppermute(block, ("x", "core", "y"), pairs)


def thirds(value):
    parts = []
    for _ in range(3):
        part = lax.reduce_precision(value, 8, 7)
        parts.append(part.astype(bf16))
        value = value - part
    return jnp.stack(parts)


def line_kernel(own, first, second, third, out):
    for z, block in enumerate((own, first, second, third)):
        value = block[...]
        for y in range(4):
            out[y, z] = value


def line_copies(*blocks):
    vmem = pl.BlockSpec(memory_space=pltpu.VMEM)
    return pl.pallas_call(
        line_kernel,
        out_shape=jax.ShapeDtypeStruct((4, 4) + blocks[0].shape, bf16),
        in_specs=[vmem] * 4,
        out_specs=vmem,
        compiler_params=pltpu.CompilerParams(vmem_limit_bytes=14 * 2**20),
        cost_estimate=pl.CostEstimate(flops=0, bytes_accessed=6 * 2**20, transcendentals=0),
    )(*blocks)


def first_kernel(place, rows, own, after_a, after_b, keep, give, keep_rows, give_rows):
    right = jnp.concatenate([own[...], after_a[...], after_b[...]], axis=0)
    where = [lax.rem(place[0] + step, 4) for step in (0, 1, 3, 2)]
    for y in range(4):
        for core, (out, rest) in enumerate(((keep, keep_rows), (give, give_rows))):
            blocks = [rows[y, z, :256, core * 256 : core * 256 + 256] for z in where]
            left = jnp.concatenate(blocks[:2], axis=1)
            out[y] = jnp.dot(left, right, preferred_element_type=f32)
            rest[y, :, :256] = blocks[2]
            rest[y, :, 256:] = blocks[3]


def first_product(place, rows, *weights):
    vmem = pl.BlockSpec(memory_space=pltpu.VMEM)
    part = jax.ShapeDtypeStruct((4, 256, 512), f32)
    left = jax.ShapeDtypeStruct((4, 256, 512), bf16)
    return pl.pallas_call(
        first_kernel,
        out_shape=(part, part, left, left),
        in_specs=[pl.BlockSpec(memory_space=pltpu.SMEM)] + [vmem] * 4,
        out_specs=(vmem,) * 4,
        compiler_params=pltpu.CompilerParams(vmem_limit_bytes=20 * 2**20),
        cost_estimate=pl.CostEstimate(
            flops=2 * 2048 * 512 * 512, bytes_accessed=11 * 2**20, transcendentals=0
        ),
    )(place, rows, *weights)


def last_kernel(part, left, before_a, before_b, far_a, far_b, out):
    pieces = (before_a, before_b, far_a, far_b)
    right = jnp.concatenate([piece[...] for piece in pieces], axis=0)
    for y in range(4):
        total = part[y] + jnp.dot(left[y], right, preferred_element_type=f32)
        out[y] = total.astype(out.dtype)


def last_product(kind, *operands):
    vmem = pl.BlockSpec(memory_space=pltpu.VMEM)
    return pl.pallas_call(
        last_kernel,
        out_shape=jax.ShapeDtypeStruct((4, 256, 512), kind),
        in_specs=[vmem] * 6,
        out_specs=vmem,
        compiler_params=pltpu.CompilerParams(vmem_limit_bytes=14 * 2**20),
        cost_estimate=pl.CostEstimate(
            flops=2048 * 512 * 512, bytes_accessed=5 * 2**20, transcendentals=0
        ),
    )(*operands)


def message_kernel(up, down, out):
    for z in range(4):
        out[z, :64] = up[...]
        out[z, 64:] = jnp.concatenate(
            [down[:, z * 2048 + x * 512 : z * 2048 + x * 512 + 512] for x in range(4)], axis=0
        )


def message(up, down):
    vmem = pl.BlockSpec(memory_space=pltpu.VMEM)
    return pl.pallas_call(
        message_kernel,
        out_shape=jax.ShapeDtypeStruct((4, 80, 512), bf16),
        in_specs=[vmem] * 2,
        out_specs=vmem,
        cost_estimate=pl.CostEstimate(flops=0, bytes_accessed=2**19, transcendentals=0),
    )(up, down)


def local(tokens, norm_gain, base_weight, factor_a, factor_b):
    core = lax.axis_index("core")
    z_hi, x = lax.axis_index("z_hi"), lax.axis_index("x")
    z_lo = lax.axis_index("z_lo")
    client = (z_hi * 4 + x) * 2 + core

    keep = lax.dynamic_slice_in_dim(tokens, core * 256, 256, axis=1)
    give = lax.dynamic_slice_in_dim(tokens, (1 - core) * 256, 256, axis=1)
    values = tokens.astype(f32)
    squares = thirds(jnp.sum(values * values, axis=1))
    squares = jnp.pad(squares, ((0, 13), (0, 256)))
    pair = jnp.concatenate([mirror(keep, 0), mirror(give, 1)], axis=1)

    both = exchange(message(factor_b.T, factor_a), "z_hi")
    up = both[:, :64].reshape(4, 4, 4, 4, 512).transpose(2, 1, 0, 3, 4).reshape(256, 512)
    down = both[:, 64:].reshape(4, 4, 4, 512).transpose(1, 0, 2, 3).reshape(4, 16, 512)
    down = jnp.broadcast_to(down[:, None], (4, 4, 16, 512)).reshape(16, 16, 512)
    pair = jnp.concatenate([pair, squares], axis=0)
    pair, up, down = lax.optimization_barrier((pair, up, down))

    rows = [ahead(pair, "z_lo", r) for r in (1, 3)]
    ups = [ahead(up, "x", r) for r in (1, 3)]
    down = copies(exchange(down, ("x", "z_lo")).reshape(256, 512))
    rows, ups, down = lax.optimization_barrier((rows, ups, down))

    rows = line_copies(pair, rows[0], ahead(pair, "z_lo", 2), rows[1])
    down = exchange(down, "y")
    up = turned([up, ups[0], ahead(up, "x", 2), ups[1]], "x")
    up = up.reshape(4, 4, 64, 512).transpose(1, 0, 2, 3).reshape(1024, 512)
    up, down = lax.optimization_barrier((up, down))

    part = lax.dot_general(
        down.reshape(1024, 512), up, (((0,), (0,)), ((), ())), preferred_element_type=f32
    )
    mine = lax.dynamic_slice_in_dim(part, core * 256, 256, axis=0)
    other = lax.dynamic_slice_in_dim(part, (1 - core) * 256, 256, axis=0).astype(bf16)
    rows, other = lax.optimization_barrier((rows, other))
    rows = exchange(rows, "y")
    update = mine + swap(other).astype(f32)
    gain = lax.dynamic_slice_in_dim(norm_gain, client * 256, 256)[:, None]
    weight = (gain * (base_weight.astype(f32) + adapter_scale * update)).astype(bf16)

    upper, lower = weight[:128], weight[128:]
    before_a, after_b = ahead(upper, "z_hi", 3), ahead(lower, "z_hi", 1)
    before_b, after_a = ahead(lower, "z_hi", 3), ahead(upper, "z_hi", 1)
    far_a, far_b = ahead(before_a, "z_hi", 3), ahead(after_b, "z_hi", 1)
    place = lax.rem(z_hi + 4 - z_lo, 4)[None]
    keep, give, keep_rows, give_rows = first_product(place, rows, weight, after_a, after_b)
    rest = (before_a, before_b, far_a, far_b)
    give = last_product(bf16, give, give_rows, *rest)
    keep = last_product(f32, keep, keep_rows, *rest)

    sums = keep + swap(give).astype(f32)
    query = jnp.sum(exchange(sums.astype(bf16), "x").astype(f32), axis=0)
    squares = jnp.sum(rows[:, :, 256:259, :256].astype(f32), axis=(0, 1, 2))
    scale = lax.rsqrt(squares / width + norm_epsilon)
    return (query * scale[:, None]).astype(bf16)


def solution(mesh):
    fine = Mesh(mesh.devices.reshape(4, 4, 2, 4, 4), ("z_hi", "x", "core", "z_lo", "y"))
    client, tensor = ("z_hi", "x", "core"), ("z_lo", "y")
    return jax.shard_map(
        local,
        mesh=fine,
        in_specs=(
            P(client, tensor),
            P(),
            P(client, tensor),
            P(client + tensor, None),
            P(tensor, client),
        ),
        out_specs=P(client, tensor),
        check_vma=False,
    )
```

```python
import jax
import jax.numpy as jnp
from jax import lax
from jax.experimental import pallas as pl
from jax.experimental.pallas import tpu as pltpu
from jax.sharding import Mesh, PartitionSpec as P

adapter_scale = 2.0
norm_epsilon = 1e-05
width = 8192

f32 = jnp.float32
bf16 = jnp.bfloat16


def exchange(blocks, axis):
    return lax.all_to_all(blocks, axis, split_axis=0, concat_axis=0)


def copies(block):
    return jnp.broadcast_to(block[None], (4,) + block.shape)


def ahead(block, axis, step):
    return lax.ppermute(block, axis, [(i, (i - step) % 4) for i in range(4)])


def turned(blocks, axis):
    return lax.dynamic_slice_in_dim(
        jnp.stack(blocks + blocks), lax.rem(4 - lax.axis_index(axis), 4), 4, axis=0
    )


def swap(block):
    return lax.ppermute(block, "core", [(0, 1), (1, 0)])


def mirror(block, flip):
    pairs = [
        ((i * 2 + c) * 4 + j, (j * 2 + (c ^ flip)) * 4 + i)
        for i in range(4)
        for c in range(2)
        for j in range(4)
    ]
    return lax.ppermute(block, ("x", "core", "y"), pairs)


def thirds(value):
    parts = []
    for _ in range(3):
        part = lax.reduce_precision(value, 8, 7)
        parts.append(part.astype(bf16))
        value = value - part
    return jnp.stack(parts)


def line_kernel(own, first, second, third, out):
    for z, block in enumerate((own, first, second, third)):
        value = block[...]
        for y in range(4):
            out[y, z] = value


def line_copies(*blocks):
    vmem = pl.BlockSpec(memory_space=pltpu.VMEM)
    return pl.pallas_call(
        line_kernel,
        out_shape=jax.ShapeDtypeStruct((4, 4) + blocks[0].shape, bf16),
        in_specs=[vmem] * 4,
        out_specs=vmem,
        compiler_params=pltpu.CompilerParams(vmem_limit_bytes=14 * 2**20),
        cost_estimate=pl.CostEstimate(flops=0, bytes_accessed=6 * 2**20, transcendentals=0),
    )(*blocks)


def first_kernel(place, rows, own, after_a, after_b, keep, give, keep_rows, give_rows):
    right = jnp.concatenate([own[...], after_a[...], after_b[...]], axis=0)
    where = [lax.rem(place[0] + step, 4) for step in (0, 1, 3, 2)]
    for y in range(4):
        for core, (out, rest) in enumerate(((keep, keep_rows), (give, give_rows))):
            blocks = [rows[y, z, :256, core * 256 : core * 256 + 256] for z in where]
            left = jnp.concatenate(blocks[:2], axis=1)
            out[y] = jnp.dot(left, right, preferred_element_type=f32)
            rest[y, :, :256] = blocks[2]
            rest[y, :, 256:] = blocks[3]


def first_product(place, rows, *weights):
    vmem = pl.BlockSpec(memory_space=pltpu.VMEM)
    part = jax.ShapeDtypeStruct((4, 256, 512), f32)
    left = jax.ShapeDtypeStruct((4, 256, 512), bf16)
    return pl.pallas_call(
        first_kernel,
        out_shape=(part, part, left, left),
        in_specs=[pl.BlockSpec(memory_space=pltpu.SMEM)] + [vmem] * 4,
        out_specs=(vmem,) * 4,
        compiler_params=pltpu.CompilerParams(vmem_limit_bytes=20 * 2**20),
        cost_estimate=pl.CostEstimate(
            flops=2 * 2048 * 512 * 512, bytes_accessed=11 * 2**20, transcendentals=0
        ),
    )(place, rows, *weights)


def last_kernel(part, left, before_a, before_b, far_a, far_b, out):
    pieces = (before_a, before_b, far_a, far_b)
    right = jnp.concatenate([piece[...] for piece in pieces], axis=0)
    for y in range(4):
        total = part[y] + jnp.dot(left[y], right, preferred_element_type=f32)
        out[y] = total.astype(out.dtype)


def last_product(kind, *operands):
    vmem = pl.BlockSpec(memory_space=pltpu.VMEM)
    return pl.pallas_call(
        last_kernel,
        out_shape=jax.ShapeDtypeStruct((4, 256, 512), kind),
        in_specs=[vmem] * 6,
        out_specs=vmem,
        compiler_params=pltpu.CompilerParams(vmem_limit_bytes=14 * 2**20),
        cost_estimate=pl.CostEstimate(
            flops=2048 * 512 * 512, bytes_accessed=5 * 2**20, transcendentals=0
        ),
    )(*operands)


def message_kernel(up, down, out):
    for z in range(4):
        out[z, :64] = up[...]
        out[z, 64:] = jnp.concatenate(
            [down[:, z * 2048 + x * 512 : z * 2048 + x * 512 + 512] for x in range(4)], axis=0
        )


def message(up, down):
    vmem = pl.BlockSpec(memory_space=pltpu.VMEM)
    return pl.pallas_call(
        message_kernel,
        out_shape=jax.ShapeDtypeStruct((4, 80, 512), bf16),
        in_specs=[vmem] * 2,
        out_specs=vmem,
        cost_estimate=pl.CostEstimate(flops=0, bytes_accessed=2**19, transcendentals=0),
    )(up, down)


def local(tokens, norm_gain, base_weight, factor_a, factor_b):
    core = lax.axis_index("core")
    z_hi, x = lax.axis_index("z_hi"), lax.axis_index("x")
    z_lo = lax.axis_index("z_lo")
    client = (z_hi * 4 + x) * 2 + core

    keep = lax.dynamic_slice_in_dim(tokens, core * 256, 256, axis=1)
    give = lax.dynamic_slice_in_dim(tokens, (1 - core) * 256, 256, axis=1)
    values = tokens.astype(f32)
    squares = thirds(jnp.sum(values * values, axis=1))
    squares = jnp.pad(squares, ((0, 13), (0, 256)))
    pair = jnp.concatenate([mirror(keep, 0), mirror(give, 1)], axis=1)

    both = exchange(message(factor_b.T, factor_a), "z_hi")
    up = both[:, :64].reshape(4, 4, 4, 4, 512).transpose(2, 1, 0, 3, 4).reshape(256, 512)
    down = both[:, 64:].reshape(4, 4, 4, 512).transpose(1, 0, 2, 3).reshape(4, 16, 512)
    down = jnp.broadcast_to(down[:, None], (4, 4, 16, 512)).reshape(16, 16, 512)
    pair = jnp.concatenate([pair, squares], axis=0)
    pair, up, down = lax.optimization_barrier((pair, up, down))

    rows = [ahead(pair, "z_lo", r) for r in (1, 3)]
    ups = [ahead(up, "x", r) for r in (1, 3)]
    down = copies(exchange(down, ("x", "z_lo")).reshape(256, 512))
    rows, ups, down = lax.optimization_barrier((rows, ups, down))

    rows = line_copies(pair, rows[0], ahead(pair, "z_lo", 2), rows[1])
    down = exchange(down, "y")
    up = turned([up, ups[0], ahead(up, "x", 2), ups[1]], "x")
    up = up.reshape(4, 4, 64, 512).transpose(1, 0, 2, 3).reshape(1024, 512)
    up, down = lax.optimization_barrier((up, down))

    down = down.reshape(1024, 512)
    other, mine = [
        lax.dot_general(
            lax.dynamic_slice_in_dim(down, place * 256, 256, axis=1),
            up,
            (((0,), (0,)), ((), ())),
            preferred_element_type=f32,
        )
        for place in (1 - core, core)
    ]
    other = other.astype(bf16)
    rows, other = lax.optimization_barrier((rows, other))
    rows = exchange(rows, "y")
    update = mine + swap(other).astype(f32)
    gain = lax.dynamic_slice_in_dim(norm_gain, client * 256, 256)[:, None]
    weight = (gain * (base_weight.astype(f32) + adapter_scale * update)).astype(bf16)

    upper, lower = weight[:128], weight[128:]
    before_a, after_b = ahead(upper, "z_hi", 3), ahead(lower, "z_hi", 1)
    before_b, after_a = ahead(lower, "z_hi", 3), ahead(upper, "z_hi", 1)
    far_a, far_b = ahead(before_a, "z_hi", 3), ahead(after_b, "z_hi", 1)
    place = lax.rem(z_hi + 4 - z_lo, 4)[None]
    keep, give, keep_rows, give_rows = first_product(place, rows, weight, after_a, after_b)
    rest = (before_a, before_b, far_a, far_b)
    give = last_product(bf16, give, give_rows, *rest)
    keep = last_product(f32, keep, keep_rows, *rest)

    sums = keep + swap(give).astype(f32)
    query = jnp.sum(exchange(sums.astype(bf16), "x").astype(f32), axis=0)
    squares = jnp.sum(rows[:, :, 256:259, :256].astype(f32), axis=(0, 1, 2))
    scale = lax.rsqrt(squares / width + norm_epsilon)
    return (query * scale[:, None]).astype(bf16)


def solution(mesh):
    fine = Mesh(mesh.devices.reshape(4, 4, 2, 4, 4), ("z_hi", "x", "core", "z_lo", "y"))
    client, tensor = ("z_hi", "x", "core"), ("z_lo", "y")
    return jax.shard_map(
        local,
        mesh=fine,
        in_specs=(
            P(client, tensor),
            P(),
            P(client, tensor),
            P(client + tensor, None),
            P(tensor, client),
        ),
        out_specs=P(client, tensor),
        check_vma=False,
    )
```

```python
import jax
import jax.numpy as jnp
from jax import lax
from jax.experimental import pallas as pl
from jax.experimental.pallas import tpu as pltpu
from jax.sharding import Mesh, PartitionSpec as P

adapter_scale = 2.0
norm_epsilon = 1e-05
width = 8192

f32 = jnp.float32
bf16 = jnp.bfloat16


def exchange(blocks, axis):
    return lax.all_to_all(blocks, axis, split_axis=0, concat_axis=0)


def copies(block):
    return jnp.broadcast_to(block[None], (4,) + block.shape)


def ahead(block, axis, step):
    return lax.ppermute(block, axis, [(i, (i - step) % 4) for i in range(4)])


def turned(blocks, axis):
    out = jnp.zeros((4,) + blocks[0].shape, blocks[0].dtype)
    for r, block in enumerate(blocks):
        place = lax.rem(lax.axis_index(axis) + r, 4)
        out = lax.dynamic_update_index_in_dim(out, block, place, 0)
    return out


def swap(block):
    return lax.ppermute(block, "core", [(0, 1), (1, 0)])


def mirror(block, flip):
    pairs = [
        ((i * 2 + c) * 4 + j, (j * 2 + (c ^ flip)) * 4 + i)
        for i in range(4)
        for c in range(2)
        for j in range(4)
    ]
    return lax.ppermute(block, ("x", "core", "y"), pairs)


def thirds(value):
    parts = []
    for _ in range(3):
        part = lax.reduce_precision(value, 8, 7)
        parts.append(part.astype(bf16))
        value = value - part
    return jnp.stack(parts)


def line_kernel(own, first, second, third, out):
    for z, block in enumerate((own, first, second, third)):
        value = block[...]
        for y in range(4):
            out[y, z] = value


def line_copies(*blocks):
    vmem = pl.BlockSpec(memory_space=pltpu.VMEM)
    return pl.pallas_call(
        line_kernel,
        out_shape=jax.ShapeDtypeStruct((4, 4) + blocks[0].shape, bf16),
        in_specs=[vmem] * 4,
        out_specs=vmem,
        compiler_params=pltpu.CompilerParams(vmem_limit_bytes=14 * 2**20),
        cost_estimate=pl.CostEstimate(flops=0, bytes_accessed=6 * 2**20, transcendentals=0),
    )(*blocks)


def first_kernel(place, rows, own, after_a, after_b, keep, give, keep_rows, give_rows):
    right = jnp.concatenate([own[...], after_a[...], after_b[...]], axis=0)
    where = [lax.rem(place[0] + step, 4) for step in (0, 1, 3, 2)]
    for y in range(4):
        for core, (out, rest) in enumerate(((keep, keep_rows), (give, give_rows))):
            blocks = [rows[y, z, :256, core * 256 : core * 256 + 256] for z in where]
            left = jnp.concatenate(blocks[:2], axis=1)
            out[y] = jnp.dot(left, right, preferred_element_type=f32)
            rest[y, :, :256] = blocks[2]
            rest[y, :, 256:] = blocks[3]


def first_product(place, rows, *weights):
    vmem = pl.BlockSpec(memory_space=pltpu.VMEM)
    part = jax.ShapeDtypeStruct((4, 256, 512), f32)
    left = jax.ShapeDtypeStruct((4, 256, 512), bf16)
    return pl.pallas_call(
        first_kernel,
        out_shape=(part, part, left, left),
        in_specs=[pl.BlockSpec(memory_space=pltpu.SMEM)] + [vmem] * 4,
        out_specs=(vmem,) * 4,
        compiler_params=pltpu.CompilerParams(vmem_limit_bytes=20 * 2**20),
        cost_estimate=pl.CostEstimate(
            flops=2 * 2048 * 512 * 512, bytes_accessed=11 * 2**20, transcendentals=0
        ),
    )(place, rows, *weights)


def last_kernel(part, left, before_a, before_b, far_a, far_b, out):
    pieces = (before_a, before_b, far_a, far_b)
    right = jnp.concatenate([piece[...] for piece in pieces], axis=0)
    for y in range(4):
        total = part[y] + jnp.dot(left[y], right, preferred_element_type=f32)
        out[y] = total.astype(out.dtype)


def last_product(kind, *operands):
    vmem = pl.BlockSpec(memory_space=pltpu.VMEM)
    return pl.pallas_call(
        last_kernel,
        out_shape=jax.ShapeDtypeStruct((4, 256, 512), kind),
        in_specs=[vmem] * 6,
        out_specs=vmem,
        compiler_params=pltpu.CompilerParams(vmem_limit_bytes=14 * 2**20),
        cost_estimate=pl.CostEstimate(
            flops=2048 * 512 * 512, bytes_accessed=5 * 2**20, transcendentals=0
        ),
    )(*operands)


def message_kernel(up, down, out):
    for z in range(4):
        out[z, :64] = up[...]
        out[z, 64:] = jnp.concatenate(
            [down[:, z * 2048 + x * 512 : z * 2048 + x * 512 + 512] for x in range(4)], axis=0
        )


def message(up, down):
    vmem = pl.BlockSpec(memory_space=pltpu.VMEM)
    return pl.pallas_call(
        message_kernel,
        out_shape=jax.ShapeDtypeStruct((4, 80, 512), bf16),
        in_specs=[vmem] * 2,
        out_specs=vmem,
        cost_estimate=pl.CostEstimate(flops=0, bytes_accessed=2**19, transcendentals=0),
    )(up, down)


def local(tokens, norm_gain, base_weight, factor_a, factor_b):
    core = lax.axis_index("core")
    z_hi, x = lax.axis_index("z_hi"), lax.axis_index("x")
    z_lo = lax.axis_index("z_lo")
    client = (z_hi * 4 + x) * 2 + core

    keep = lax.dynamic_slice_in_dim(tokens, core * 256, 256, axis=1)
    give = lax.dynamic_slice_in_dim(tokens, (1 - core) * 256, 256, axis=1)
    values = tokens.astype(f32)
    squares = thirds(jnp.sum(values * values, axis=1))
    squares = jnp.pad(squares, ((0, 13), (0, 256)))
    pair = jnp.concatenate([mirror(keep, 0), mirror(give, 1)], axis=1)

    both = exchange(message(factor_b.T, factor_a), "z_hi")
    up = both[:, :64].reshape(4, 4, 4, 4, 512).transpose(2, 1, 0, 3, 4).reshape(256, 512)
    down = both[:, 64:].reshape(4, 4, 4, 512).transpose(1, 0, 2, 3).reshape(4, 16, 512)
    down = jnp.broadcast_to(down[:, None], (4, 4, 16, 512)).reshape(16, 16, 512)
    pair = jnp.concatenate([pair, squares], axis=0)
    pair, up, down = lax.optimization_barrier((pair, up, down))

    rows = [ahead(pair, "z_lo", r) for r in (1, 3)]
    ups = [ahead(up, "x", r) for r in (1, 3)]
    down = copies(exchange(down, ("x", "z_lo")).reshape(256, 512))
    rows, ups, down = lax.optimization_barrier((rows, ups, down))

    rows = line_copies(pair, rows[0], ahead(pair, "z_lo", 2), rows[1])
    down = exchange(down, "y")
    up = turned([up, ups[0], ahead(up, "x", 2), ups[1]], "x")
    up = up.reshape(4, 4, 64, 512).transpose(1, 0, 2, 3).reshape(1024, 512)
    up, down = lax.optimization_barrier((up, down))

    down = down.reshape(1024, 512)
    other, mine = [
        lax.dot_general(
            lax.dynamic_slice_in_dim(down, place * 256, 256, axis=1),
            up,
            (((0,), (0,)), ((), ())),
            preferred_element_type=f32,
        )
        for place in (1 - core, core)
    ]
    other = other.astype(bf16)
    rows, other = lax.optimization_barrier((rows, other))
    rows = exchange(rows, "y")
    update = mine + swap(other).astype(f32)
    gain = lax.dynamic_slice_in_dim(norm_gain, client * 256, 256)[:, None]
    weight = (gain * (base_weight.astype(f32) + adapter_scale * update)).astype(bf16)

    upper, lower = weight[:128], weight[128:]
    before_a, after_b = ahead(upper, "z_hi", 3), ahead(lower, "z_hi", 1)
    before_b, after_a = ahead(lower, "z_hi", 3), ahead(upper, "z_hi", 1)
    far_a, far_b = ahead(before_a, "z_hi", 3), ahead(after_b, "z_hi", 1)
    place = lax.rem(z_hi + 4 - z_lo, 4)[None]
    keep, give, keep_rows, give_rows = first_product(place, rows, weight, after_a, after_b)
    rest = (before_a, before_b, far_a, far_b)
    give = last_product(bf16, give, give_rows, *rest)
    keep = last_product(f32, keep, keep_rows, *rest)

    sums = keep + swap(give).astype(f32)
    query = jnp.sum(exchange(sums.astype(bf16), "x").astype(f32), axis=0)
    squares = jnp.sum(rows[:, :, 256:259, :256].astype(f32), axis=(0, 1, 2))
    scale = lax.rsqrt(squares / width + norm_epsilon)
    return (query * scale[:, None]).astype(bf16)


def solution(mesh):
    fine = Mesh(mesh.devices.reshape(4, 4, 2, 4, 4), ("z_hi", "x", "core", "z_lo", "y"))
    client, tensor = ("z_hi", "x", "core"), ("z_lo", "y")
    return jax.shard_map(
        local,
        mesh=fine,
        in_specs=(
            P(client, tensor),
            P(),
            P(client, tensor),
            P(client + tensor, None),
            P(tensor, client),
        ),
        out_specs=P(client, tensor),
        check_vma=False,
    )
```
